256 devices in a mesh: pq: 16 (over z_hi, x), rs: 16 (over y, z_lo, core).
Axes of the slice: x: 4, y: 4, z: 8 (z_hi: 4, z_lo: 2; z = z_hi * 2 + z_lo), core: 2. Of those that a mesh axis runs over, the one named last changes fastest.
Arguments:
- integrals: bfloat16 [2, 8192, 65536], P(None, 'pq', 'rs'), may hold values from -6 to 6
- screen: int32 [2, 64, 512], P(None, 'pq', 'rs'), may hold values 0 or 1
- rs_coeff: bfloat16 [65536, 1024], P('rs', 'pq'), may hold values from -0.0234375 to 0.0234375
- pq_coeff: bfloat16 [2, 8192, 1024], P(None, 'pq'), may hold values from -0.0625 to 0.0625
Outputs:
- ovov: float32 [2, 1024, 1024], P(None, 'pq', 'rs')
The draws below stay inside these ranges and needn't reach their ends.
Inputs may be any that keep to these rules, and one draw needn't show every extreme that they name: `screen`: 1 where a tile survives screening, 0 where it is dropped.
All inputs are finite; a program needn't handle non-finite values. No bound on the sum of `screen` on one device may be relied on, other than what follows from the above.
Results may differ from the reference program's by a relative error of at most 0.0029.
Values may be sent and summed in bfloat16 or wider, within the bound.
No kernel may reach another device: no remote copies, remote signals or barrier semaphores. Data moves between devices by JAX's collectives and lax.ppermute only.
A program may use at most 128 MiB of HBM per device.

```python
import jax
import jax.numpy as jnp
from jax import lax

TILE = 128
SLABS = 2
OVA = 1024
OVB = 1024
PQ = 8192
RS = 65536


def with_ends(drawn, rng, least, high):
    longest = drawn.shape.index(max(drawn.shape))
    spots = []
    for shift in (0, 1):
        where = [jax.random.randint(jax.random.fold_in(rng, axis), (), 0, length) for axis, length in enumerate(drawn.shape)]
        where[longest] = (where[longest] + shift) % drawn.shape[longest]
        spots.append(tuple(where))
    return drawn.at[spots[0]].set(least).at[spots[1]].set(high)


def levels(key, extent, shards, smallest, top_value):
    gain, own = 1.0, jax.random.fold_in(key, 6)
    for axis_at, shards_of in shards:
        heights = jnp.exp(jax.random.uniform(jax.random.fold_in(own, axis_at), (shards_of,), jnp.float32, smallest / len(shards), top_value / len(shards)))
        gain = gain * jnp.repeat(heights, extent[axis_at] // shards_of).reshape([-1 if axis == axis_at else 1 for axis in range(len(extent))])
    return gain


def bell_draw(key, dims, deviation, limit, pieces=(), dtype=jnp.bfloat16):
    gain = levels(key, dims, pieces, -0.22, 0.18) if pieces else 1.0
    array = jax.random.normal(key, dims, jnp.float32) * deviation * gain
    return jnp.minimum(jnp.maximum(array, -limit), limit).astype(dtype)


def setup_inputs(seed: int = 0) -> dict:
    key_list = jax.random.split(jax.random.key(seed), 5)
    return {
        "integrals": bell_draw(key_list[0], (SLABS, PQ, RS), 1.0, 6.0, ((1, 16), (2, 16))),
        "screen": with_ends((jax.random.randint(key_list[1], (SLABS, PQ // TILE, RS // TILE), 0, 4) < 3).astype(jnp.int32), jax.random.fold_in(key_list[1], 1), 0, 1),
        "rs_coeff": bell_draw(key_list[2], (RS, OVB), RS ** -0.5, 0.0234375, ((0, 16), (1, 16))),
        "pq_coeff": bell_draw(key_list[3], (SLABS, PQ, OVA), PQ ** -0.5, 0.0625, ((1, 16),)),
    }


def reference(integrals, screen, rs_coeff, pq_coeff):
    results = []
    for index_slab in range(SLABS):
        row_blocks = integrals[index_slab].reshape(PQ // TILE, TILE, RS)
        flags = screen[index_slab].astype(jnp.bfloat16)

        def one_block(pair):
            block_rows, flag_row = pair
            shaped = block_rows.reshape(TILE, RS // TILE, TILE) * flag_row[None, :, None]
            return jnp.dot(shaped.reshape(TILE, RS), rs_coeff, preferred_element_type=jnp.float32)

        partial_value = lax.map(one_block, (row_blocks, flags)).reshape(PQ, OVB)
        half = partial_value.astype(jnp.bfloat16)
        results.append(jnp.dot(pq_coeff[index_slab].T, half, preferred_element_type=jnp.float32))
    return jnp.stack(results)
```

```python
import functools

import jax
import jax.numpy as jnp
from jax import lax
from jax.experimental import pallas as pl
from jax.experimental.pallas import tpu as pltpu
from jax.sharding import PartitionSpec as P

TILE = 128
F32 = jnp.float32
BF16 = jnp.bfloat16
VMEM_LIMIT = 40 * 1024 * 1024


def pq_shift(value, dz, dx):
    perm = []
    for index in range(16):
        z, x = divmod(index, 4)
        perm.append((index, (z + dz) % 4 * 4 + (x + dx) % 4))
    return lax.ppermute(value, "pq", perm)


def core_swap(value):
    return lax.ppermute(value, "rs", [(index, index ^ 1) for index in range(16)])


def params():
    return pltpu.CompilerParams(vmem_limit_bytes=VMEM_LIMIT)


def cost(flops, bytes_accessed):
    return pl.CostEstimate(flops=flops, bytes_accessed=bytes_accessed, transcendentals=0)


def mask_kernel(screen_ref, a_ref, out_ref):
    row = pl.program_id(0)
    for col in range(a_ref.shape[1] // TILE):
        flag = screen_ref[row, col].astype(F32)
        at = slice(col * TILE, (col + 1) * TILE)
        out_ref[:, at] = (a_ref[:, at].astype(F32) * flag).astype(BF16)


def mask(integrals, screen):
    rows, cols = integrals.shape
    return pl.pallas_call(
        mask_kernel,
        out_shape=jax.ShapeDtypeStruct((rows, cols), BF16),
        grid_spec=pltpu.PrefetchScalarGridSpec(
            num_scalar_prefetch=1,
            grid=(rows // TILE,),
            in_specs=[pl.BlockSpec((TILE, cols), lambda row, _: (row, 0))],
            out_specs=pl.BlockSpec((TILE, cols), lambda row, _: (row, 0)),
        ),
        compiler_params=params(),
        cost_estimate=cost(rows * cols, 4 * rows * cols),
    )(screen, integrals)


def half_kernel(counts, swap_ref, a_ref, *refs):
    pieces, (keep_ref, send_ref) = refs[:-2], refs[-2:]
    a = a_ref[...]

    def product(some):
        value = jnp.concatenate([ref[...] for ref in some], axis=0)
        return lax.dot_general(value, a, (((1,), (1,)), ((), ())), preferred_element_type=F32)

    even = product(pieces[: counts[0]])
    odd = product(pieces[counts[0] :])
    swap = swap_ref[0] != 0
    keep_ref[...] = jnp.where(swap, odd, even)
    send_ref[...] = jnp.where(swap, even, odd)


def half_transform(swap, masked, even, odd):
    rows, cols = masked.shape
    width = 256
    n = sum(piece.shape[0] for piece in even)
    pieces = list(even) + list(odd)
    out = jax.ShapeDtypeStruct((n, rows), F32)
    return pl.pallas_call(
        functools.partial(half_kernel, (len(even), len(odd))),
        out_shape=[out, out],
        grid_spec=pltpu.PrefetchScalarGridSpec(
            num_scalar_prefetch=1,
            grid=(rows // width,),
            in_specs=[pl.BlockSpec((width, cols), lambda at, _: (at, 0))]
            + [pl.BlockSpec(piece.shape, lambda at, _: (0, 0)) for piece in pieces],
            out_specs=[pl.BlockSpec((n, width), lambda at, _: (0, at))] * 2,
        ),
        compiler_params=params(),
        cost_estimate=cost(4 * n * rows * cols, 2 * rows * cols + 4 * n * cols + 8 * n * rows),
    )(swap, masked, *pieces)


def pack_kernel(dest_ref, *refs):
    out_ref = refs[-1]
    slot = 0
    for at in range(0, len(refs) - 1, 2):
        keep_ref, got_ref = refs[at], refs[at + 1]
        for first in range(0, keep_ref.shape[0], 64):
            rows = slice(first, first + 64)
            out_ref[dest_ref[slot]] = (keep_ref[rows, :] + got_ref[rows, :]).astype(BF16)
            slot += 1


def pack(dest, pairs):
    flat = [value for pair in pairs for value in pair]
    rows = flat[0].shape[1]
    return pl.pallas_call(
        pack_kernel,
        out_shape=jax.ShapeDtypeStruct((8, 64, rows), BF16),
        in_specs=[pl.BlockSpec(memory_space=pltpu.SMEM)]
        + [pl.BlockSpec(memory_space=pltpu.VMEM)] * len(flat),
        out_specs=pl.BlockSpec(memory_space=pltpu.VMEM),
        compiler_params=params(),
        cost_estimate=cost(8 * 64 * rows, 10 * 8 * 64 * rows),
    )(dest, *flat)


def second_kernel(x_ref, got_ref, coeff_ref, *refs):
    outs, turned_ref = refs[:-1], refs[-1]
    half = got_ref[0].astype(F32)
    for at in range(1, 8):
        half = half + got_ref[at].astype(F32)
    high = half.astype(BF16)
    low = (half - high.astype(F32)).astype(BF16)
    parts = []
    for slab in range(2):
        at = slice(slab * 512, (slab + 1) * 512)
        coeff = coeff_ref[slab]
        both = jnp.concatenate([high[:, at], low[:, at]], axis=0)
        product = jnp.dot(both, coeff, preferred_element_type=F32)
        parts.append(product[:64] + product[64:])
    turned_ref[...] = jnp.concatenate(parts, axis=0).T
    for dx in range(4):
        x = lax.rem(x_ref[0] + dx, 4)
        for z in range(4):
            first = pl.multiple_of((z * 4 + x) * 64, 64)
            outs[dx][z] = turned_ref[pl.ds(first, 64), :]


def second_transform(x, got, pq_coeff):
    out = jax.ShapeDtypeStruct((4, 64, 128), F32)
    return pl.pallas_call(
        second_kernel,
        out_shape=[out] * 4,
        in_specs=[pl.BlockSpec(memory_space=pltpu.SMEM)]
        + [pl.BlockSpec(memory_space=pltpu.VMEM)] * 2,
        out_specs=[pl.BlockSpec(memory_space=pltpu.VMEM)] * 4,
        scratch_shapes=[pltpu.VMEM((1024, 128), F32)],
        compiler_params=params(),
        cost_estimate=cost(8 * 64 * 512 * 1024, 4 * 1024 * 1024),
    )(x, got, pq_coeff)


def turn_kernel(z_ref, a_ref, b_ref, c_ref, d_ref, *outs):
    for dz in range(4):
        z = lax.rem(z_ref[0] + dz, 4)
        outs[dz][...] = (a_ref[z] + b_ref[z]) + (c_ref[z] + d_ref[z])


def turn(z, parts):
    out = jax.ShapeDtypeStruct((64, 128), F32)
    return pl.pallas_call(
        turn_kernel,
        out_shape=[out] * 4,
        in_specs=[pl.BlockSpec(memory_space=pltpu.SMEM)]
        + [pl.BlockSpec(memory_space=pltpu.VMEM)] * 4,
        out_specs=[pl.BlockSpec(memory_space=pltpu.VMEM)] * 4,
        compiler_params=params(),
        cost_estimate=cost(4 * 64 * 128 * 4, 4 * 64 * 128 * 4 * 5),
    )(z, *parts)


def last_kernel(a_ref, b_ref, c_ref, d_ref, out_ref):
    total = (a_ref[...] + b_ref[...]) + (c_ref[...] + d_ref[...])
    out_ref[0] = total[:, :64]
    out_ref[1] = total[:, 64:]


def last(parts):
    return pl.pallas_call(
        last_kernel,
        out_shape=jax.ShapeDtypeStruct((2, 64, 64), F32),
        in_specs=[pl.BlockSpec(memory_space=pltpu.VMEM)] * 4,
        out_specs=pl.BlockSpec(memory_space=pltpu.VMEM),
        compiler_params=params(),
    )(*parts)


def body(integrals, screen, rs_coeff, pq_coeff):
    slabs, pq_rows, rs_cols = integrals.shape
    pq_at, rs_at = lax.axis_index("pq"), lax.axis_index("rs")
    z, x = pq_at // 4, pq_at % 4
    core = rs_at % 2
    swap = (x + core) % 2

    own = rs_coeff.T
    top, low = slice(0, 32), slice(32, 64)

    z_less = pq_shift(own, 1, 0)
    z_more = pq_shift(own, -1, 0)
    x_less = pq_shift(own, 0, 1)
    x_more = pq_shift(own, 0, -1)
    masked = mask(
        integrals.reshape(slabs * pq_rows, rs_cols),
        screen.reshape(slabs * (pq_rows // TILE), rs_cols // TILE),
    )
    x_two = jnp.concatenate(
        [pq_shift(x_less[top], 0, 1), pq_shift(x_more[low], 0, -1)], axis=0
    )
    z_two = jnp.concatenate(
        [pq_shift(z_less[top], 1, 0), pq_shift(z_more[low], -1, 0)], axis=0
    )
    more_less = pq_shift(z_more, 0, 1)
    more_more = pq_shift(z_more, 0, -1)
    less_two = pq_shift(x_two, 1, 0)
    more_two = pq_shift(x_two, -1, 0)
    two_less = pq_shift(z_two, 0, 1)
    two_more = pq_shift(z_two, 0, -1)
    less_less = pq_shift(z_less, 0, 1)
    less_more = pq_shift(z_less, 0, -1)
    two_two_top = pq_shift(two_less[top], 0, 1)
    two_two_low = pq_shift(two_more[low], 0, -1)

    groups = [
        ([own, x_two], [x_less, x_more], [(0, 0), (0, 2)], [(0, -1), (0, 1)]),
        ([z_less, z_more], [more_less, more_more], [(-1, 0), (1, 0)], [(1, -1), (1, 1)]),
        ([z_two], [two_less], [(2, 0)], [(2, -1)]),
        (
            [less_two, more_two, two_two_top, two_two_low],
            [two_more, less_less, less_more],
            [(-1, 2), (1, 2), (2, 2)],
            [(2, 1), (-1, -1), (-1, 1)],
        ),
    ]
    swap_at = swap.astype(jnp.int32).reshape(1)
    pairs, dest = [], []
    for even, odd, even_at, odd_at in groups:
        keep, send = half_transform(swap_at, masked, even, odd)
        pairs.append((keep, core_swap(send)))
        for (ez, ex), (oz, ox) in zip(even_at, odd_at):
            dz, dx = jnp.where(swap == 0, ez, oz), jnp.where(swap == 0, ex, ox)
            dest.append((z + dz + 4) % 4 * 2 + (x + dx + 4) % 4 // 2)
    packed = pack(jnp.stack(dest).astype(jnp.int32), pairs)
    got = lax.all_to_all(
        packed,
        "rs",
        0,
        0,
        tiled=True,
        axis_index_groups=[[index * 2 + at for index in range(8)] for at in range(2)],
    )
    parts = second_transform(x.astype(jnp.int32).reshape(1), got, pq_coeff)
    parts = [parts[0]] + [pq_shift(parts[dx], 0, dx) for dx in (1, 2, 3)]
    parts = turn(z.astype(jnp.int32).reshape(1), parts)
    parts = [parts[0]] + [pq_shift(parts[dz], dz, 0) for dz in (1, 2, 3)]
    return last(parts)


def solution(mesh):
    return jax.shard_map(
        body,
        mesh=mesh,
        in_specs=(P(None, "pq", "rs"), P(None, "pq", "rs"), P("rs", "pq"), P(None, "pq", None)),
        out_specs=P(None, "pq", "rs"),
        check_vma=False,
    )
```

```python
import functools

import jax
import jax.numpy as jnp
from jax import lax
from jax.experimental import pallas as pl
from jax.experimental.pallas import tpu as pltpu
from jax.sharding import PartitionSpec as P

TILE = 128
F32 = jnp.float32
BF16 = jnp.bfloat16
VMEM_LIMIT = 14 * 1024 * 1024
WIDTH = 256
TOKEN = jax.ShapeDtypeStruct((8, 128), F32)


def pq_shift(value, dz, dx):
    perm = []
    for index in range(16):
        z, x = divmod(index, 4)
        perm.append((index, (z + dz) % 4 * 4 + (x + dx) % 4))
    return lax.ppermute(value, "pq", perm)


def send(value, dz, dx):
    perm = []
    for index in range(256):
        pq_at, rs_at = divmod(index, 16)
        z, x = divmod(pq_at, 4)
        sign = 1 if rs_at % 2 == 0 else -1
        perm.append((index, ((z + sign * dz) % 4 * 4 + (x + sign * dx) % 4) * 16 + rs_at))
    return lax.ppermute(value, ("pq", "rs"), perm)


def after(value, *others):
    return lax.optimization_barrier((value,) + others)[0]


SHIFTS = [(0, 0), (0, 1), (1, 0), (1, 1), (2, 0), (2, 1), (3, 0), (3, 1)]


def rs_send(value, dy, dl):
    perm = []
    for index in range(16):
        y, rest = divmod(index, 4)
        sign = 1 if index % 2 == 0 else -1
        perm.append((index, (y + sign * dy) % 4 * 4 + rest ^ (dl * 2)))
    return lax.ppermute(value, "rs", perm)


def core_swap(value):
    return lax.ppermute(value, "rs", [(index, index ^ 1) for index in range(16)])


def params():
    return pltpu.CompilerParams(vmem_limit_bytes=VMEM_LIMIT)


def cost(flops, bytes_accessed):
    return pl.CostEstimate(flops=flops, bytes_accessed=bytes_accessed, transcendentals=0)


def mask_kernel(screen_ref, a_ref, out_ref, token_ref):
    at = pl.program_id(0)
    token_ref[...] = jnp.zeros(token_ref.shape, F32)
    for col in range(a_ref.shape[1] // TILE):
        cols = slice(col * TILE, (col + 1) * TILE)
        for row in range(WIDTH // TILE):
            rows = slice(row * TILE, (row + 1) * TILE)
            flag = screen_ref[at * (WIDTH // TILE) + row, col].astype(F32)
            out_ref[0, cols, rows] = (a_ref[rows, cols].astype(F32) * flag).T.astype(BF16)


def mask(integrals, screen):
    rows, cols = integrals.shape
    return pl.pallas_call(
        mask_kernel,
        out_shape=[jax.ShapeDtypeStruct((rows // WIDTH, cols, WIDTH), BF16), TOKEN],
        grid_spec=pltpu.PrefetchScalarGridSpec(
            num_scalar_prefetch=1,
            grid=(rows // WIDTH,),
            in_specs=[pl.BlockSpec((WIDTH, cols), lambda at, _: (at, 0))],
            out_specs=[
                pl.BlockSpec((1, cols, WIDTH), lambda at, _: (at, 0, 0)),
                pl.BlockSpec(TOKEN.shape, lambda at, _: (0, 0)),
            ],
        ),
        compiler_params=params(),
        cost_estimate=cost(rows * cols, 4 * rows * cols),
    )(screen, integrals)


def half_kernel(swap_ref, a_ref, *refs):
    pieces, (keep_ref, send_ref) = refs[:4], refs[-2:]
    n = keep_ref.shape[0]
    swap = swap_ref[0] != 0
    coeff = jnp.concatenate([ref[...] for ref in pieces], axis=0)
    for at in range(a_ref.shape[0]):
        cols = slice(at * WIDTH, (at + 1) * WIDTH)
        product = jnp.dot(coeff, a_ref[at], preferred_element_type=F32)
        even, odd = product[:n], product[n:]
        keep_ref[:, cols] = jnp.where(swap, odd, even)
        send_ref[:, cols] = jnp.where(swap, even, odd)


def half_transform(swap, masked, even, odd, waits=()):
    count, cols, width = masked.shape
    rows = count * width
    pieces = list(even) + list(odd)
    n = len(even) * 64
    out = jax.ShapeDtypeStruct((n, rows), F32)
    return pl.pallas_call(
        half_kernel,
        out_shape=[out, out],
        in_specs=[pl.BlockSpec(memory_space=pltpu.SMEM)]
        + [pl.BlockSpec(memory_space=pltpu.VMEM)] * (1 + len(pieces))
        + [pl.BlockSpec(memory_space=pl.ANY)] * len(waits),
        out_specs=[pl.BlockSpec(memory_space=pltpu.VMEM)] * 2,
        compiler_params=params(),
        cost_estimate=cost(4 * n * rows * cols, 2 * rows * cols + 4 * n * cols + 8 * n * rows),
    )(swap, masked, *pieces, *waits)


def pack_kernel(keep_at_ref, got_at_ref, *refs):
    inputs, outs, total_ref = refs[:8], refs[8:16], refs[16]
    for at in range(4):
        for row in range(2):
            rows = slice(row * 64, (row + 1) * 64)
            total_ref[keep_at_ref[at * 2 + row]] = inputs[at * 2][rows, :]
    for at in range(4):
        for row in range(2):
            rows = slice(row * 64, (row + 1) * 64)
            total_ref[got_at_ref[at * 2 + row]] += inputs[at * 2 + 1][rows, :]
    for at in range(8):
        outs[at][...] = total_ref[at].astype(outs[at].dtype)


def pack(keep_at, got_at, pairs):
    flat = [value for pair in pairs for value in pair]
    rows = flat[0].shape[1]
    return pl.pallas_call(
        pack_kernel,
        out_shape=[jax.ShapeDtypeStruct((64, rows), F32 if at == 0 else BF16) for at in range(8)],
        in_specs=[pl.BlockSpec(memory_space=pltpu.SMEM)] * 2
        + [pl.BlockSpec(memory_space=pltpu.VMEM)] * 8,
        out_specs=[pl.BlockSpec(memory_space=pltpu.VMEM)] * 8,
        scratch_shapes=[pltpu.VMEM((8, 64, rows), F32)],
        compiler_params=params(),
        cost_estimate=cost(8 * 64 * rows, 10 * 8 * 64 * rows),
    )(keep_at, got_at, *flat)


def second_kernel(x_ref, *refs):
    gots, coeff_ref, outs, turned_ref = refs[:8], refs[8], refs[9:13], refs[13]
    half = gots[0][...]
    for ref in gots[1:]:
        half = half + ref[...].astype(F32)
    high = half.astype(BF16)
    low = (half - high.astype(F32)).astype(BF16)
    parts = []
    for slab in range(2):
        at = slice(slab * 512, (slab + 1) * 512)
        coeff = coeff_ref[slab]
        both = jnp.concatenate([high[:, at], low[:, at]], axis=0)
        product = jnp.dot(both, coeff, preferred_element_type=F32)
        parts.append(product[:64] + product[64:])
    turned_ref[...] = jnp.concatenate(parts, axis=0).T
    for dx in range(4):
        x = lax.rem(x_ref[0] + dx, 4)
        for z in range(4):
            first = pl.multiple_of((z * 4 + x) * 64, 64)
            outs[dx][z] = turned_ref[pl.ds(first, 64), :].astype(outs[dx].dtype)


def second_transform(x, gots, pq_coeff):
    return pl.pallas_call(
        second_kernel,
        out_shape=[jax.ShapeDtypeStruct((4, 64, 128), F32) for at in range(4)],
        in_specs=[pl.BlockSpec(memory_space=pltpu.SMEM)]
        + [pl.BlockSpec(memory_space=pltpu.VMEM)] * 9,
        out_specs=[pl.BlockSpec(memory_space=pltpu.VMEM)] * 4,
        scratch_shapes=[pltpu.VMEM((1024, 128), F32)],
        compiler_params=params(),
        cost_estimate=cost(8 * 64 * 512 * 1024, 4 * 1024 * 1024),
    )(x, *gots, pq_coeff)


def turn_kernel(z_ref, a_ref, b_ref, c_ref, d_ref, *outs):
    for dz in range(4):
        z = lax.rem(z_ref[0] + dz, 4)
        near = b_ref[z].astype(F32) + c_ref[z].astype(F32)
        outs[dz][...] = a_ref[z] + (near + d_ref[z].astype(F32))


def turn(z, parts):
    out = jax.ShapeDtypeStruct((64, 128), F32)
    return pl.pallas_call(
        turn_kernel,
        out_shape=[out] * 4,
        in_specs=[pl.BlockSpec(memory_space=pltpu.SMEM)]
        + [pl.BlockSpec(memory_space=pltpu.VMEM)] * 4,
        out_specs=[pl.BlockSpec(memory_space=pltpu.VMEM)] * 4,
        compiler_params=params(),
        cost_estimate=cost(4 * 64 * 128 * 4, 4 * 64 * 128 * 4 * 5),
    )(z, *parts)


def last_kernel(a_ref, b_ref, c_ref, d_ref, out_ref):
    total = (a_ref[...] + b_ref[...]) + (c_ref[...] + d_ref[...])
    out_ref[0] = total[:, :64]
    out_ref[1] = total[:, 64:]


def last(parts):
    return pl.pallas_call(
        last_kernel,
        out_shape=jax.ShapeDtypeStruct((2, 64, 64), F32),
        in_specs=[pl.BlockSpec(memory_space=pltpu.VMEM)] * 4,
        out_specs=pl.BlockSpec(memory_space=pltpu.VMEM),
        compiler_params=params(),
    )(*parts)


def body(integrals, screen, rs_coeff, pq_coeff):
    slabs, pq_rows, rs_cols = integrals.shape
    pq_at, rs_at = lax.axis_index("pq"), lax.axis_index("rs")
    z, x = pq_at // 4, pq_at % 4
    core = rs_at % 2
    sign = 1 - 2 * core
    swap = (x + core) % 2
    swap_at = swap.astype(jnp.int32).reshape(1)

    own = rs_coeff.T

    block = {(0, 0): own}
    block[0, -1] = send(own, 0, 1)
    block[-1, 0] = send(own, 1, 0)
    block[0, 1] = send(own, 0, -1)
    masked, token = mask(
        integrals.reshape(slabs * pq_rows, rs_cols),
        screen.reshape(slabs * (pq_rows // TILE), rs_cols // TILE),
    )
    x_less, token = lax.optimization_barrier((block[0, -1], token))
    block[0, 2] = send(x_less, 0, 1)
    block[2, 0] = send(block[-1, 0], 1, 0)
    block[-1, -1] = send(after(block[-1, 0], block[0, -1]), 0, 1)
    block[-1, 1] = send(after(block[-1, 0], block[0, 1]), 0, -1)
    block[-1, 2] = send(block[-1, -1], 0, 1)
    block[1, 0] = send(after(own, block[0, 2]), -1, 0)
    first = half_transform(
        swap_at, masked, [own, block[0, 2]], [block[0, -1], block[0, 1]], [token]
    )
    block[2, -1] = send(after(block[2, 0], block[0, 2]), 0, 1)
    block[2, 1] = send(after(block[2, 0], block[-1, -1]), 0, -1)
    block[2, 2] = send(after(block[2, -1], block[-1, 2], block[-1, 1], *first), 0, 1)
    block[1, 2] = send(after(block[0, 2], block[1, 0]), -1, 0)
    block[1, -1] = send(after(block[1, 0], block[2, -1]), 0, 1)
    block[1, 1] = send(after(block[1, 0], block[2, 1]), 0, -1)
    second = half_transform(
        swap_at, masked, [block[-1, 0], block[-1, 2]], [block[-1, -1], block[-1, 1]], first
    )
    third = half_transform(
        swap_at, masked, [block[2, 0], block[2, 2]], [block[2, -1], block[2, 1]], second
    )
    fourth = half_transform(
        swap_at, masked, [block[1, 0], block[1, 2]], [block[1, -1], block[1, 1]], third
    )
    halves = [first, second, third, fourth]
    places = [((dz, even), (dz, odd)) for dz in (0, -1, 2, 1) for even, odd in ((0, -1), (2, 1))]

    def slot(place, sign):
        to = (z + sign * place[0] + 4) % 4, (x + sign * place[1] + 4) % 4
        shift = (one * (to[0] - y) + 8) % 4 * 2 + (to[1] // 2 - low + 2) % 2
        return sum(
            jnp.where(shift == dy * 2 + dl, at, 0) for at, (dy, dl) in enumerate(SHIFTS)
        )

    one = sign
    y, low = rs_at // 4, rs_at % 4 // 2
    keep_at = jnp.stack([jnp.where(swap == 0, slot(e, one), slot(o, one)) for e, o in places])
    got_at = jnp.stack([jnp.where(swap == 0, slot(e, -one), slot(o, -one)) for e, o in places])
    pairs = [(keep, core_swap(other)) for keep, other in halves]
    gots = list(pack(keep_at.astype(jnp.int32), got_at.astype(jnp.int32), pairs))
    for at in range(1, 8):
        gots[at] = rs_send(gots[at], *SHIFTS[at])
    parts = second_transform(x.astype(jnp.int32).reshape(1), gots, pq_coeff)
    parts = [parts[0]] + [pq_shift(parts[dx], 0, dx) for dx in (1, 2, 3)]
    parts = turn(z.astype(jnp.int32).reshape(1), parts)
    parts = [parts[0]] + [pq_shift(parts[dz], dz, 0) for dz in (1, 2, 3)]
    return last(parts)


def solution(mesh):
    return jax.shard_map(
        body,
        mesh=mesh,
        in_specs=(P(None, "pq", "rs"), P(None, "pq", "rs"), P("rs", "pq"), P(None, "pq", None)),
        out_specs=P(None, "pq", "rs"),
        check_vma=False,
    )
```

```python
import functools

import jax
import jax.numpy as jnp
from jax import lax
from jax.experimental import pallas as pl
from jax.experimental.pallas import tpu as pltpu
from jax.sharding import PartitionSpec as P

TILE = 128
F32 = jnp.float32
BF16 = jnp.bfloat16
VMEM_LIMIT = 14 * 1024 * 1024
WIDTH = 256


def pq_shift(value, dz, dx):
    perm = []
    for index in range(16):
        z, x = divmod(index, 4)
        perm.append((index, (z + dz) % 4 * 4 + (x + dx) % 4))
    return lax.ppermute(value, "pq", perm)


def send(value, dz, dx):
    perm = []
    for index in range(256):
        pq_at, rs_at = divmod(index, 16)
        z, x = divmod(pq_at, 4)
        sign = 1 if rs_at % 2 == 0 else -1
        perm.append((index, ((z + sign * dz) % 4 * 4 + (x + sign * dx) % 4) * 16 + rs_at))
    return lax.ppermute(value, ("pq", "rs"), perm)


def after(value, *others):
    return lax.optimization_barrier((value,) + others)[0]


SHIFTS = [(0, 0), (0, 1), (1, 0), (1, 1), (2, 0), (2, 1), (3, 0), (3, 1)]


def rs_send(value, dy, dl):
    perm = []
    for index in range(16):
        y, rest = divmod(index, 4)
        sign = 1 if index % 2 == 0 else -1
        perm.append((index, (y + sign * dy) % 4 * 4 + rest ^ (dl * 2)))
    return lax.ppermute(value, "rs", perm)


def core_swap(value):
    return lax.ppermute(value, "rs", [(index, index ^ 1) for index in range(16)])


def params():
    return pltpu.CompilerParams(vmem_limit_bytes=VMEM_LIMIT)


def cost(flops, bytes_accessed):
    return pl.CostEstimate(flops=flops, bytes_accessed=bytes_accessed, transcendentals=0)


def mask_kernel(screen_ref, a_ref, out_ref):
    at = pl.program_id(0)
    for col in range(a_ref.shape[1] // TILE):
        cols = slice(col * TILE, (col + 1) * TILE)
        for row in range(WIDTH // TILE):
            rows = slice(row * TILE, (row + 1) * TILE)
            flag = screen_ref[at * (WIDTH // TILE) + row, col].astype(F32)
            out_ref[0, cols, rows] = (a_ref[rows, cols].astype(F32) * flag).T.astype(BF16)


def mask(integrals, screen):
    rows, cols = integrals.shape
    return pl.pallas_call(
        mask_kernel,
        out_shape=jax.ShapeDtypeStruct((rows // WIDTH, cols, WIDTH), BF16),
        grid_spec=pltpu.PrefetchScalarGridSpec(
            num_scalar_prefetch=1,
            grid=(rows // WIDTH,),
            in_specs=[pl.BlockSpec((WIDTH, cols), lambda at, _: (at, 0))],
            out_specs=pl.BlockSpec((1, cols, WIDTH), lambda at, _: (at, 0, 0)),
        ),
        compiler_params=params(),
        cost_estimate=cost(rows * cols, 4 * rows * cols),
    )(screen, integrals)


def half_kernel(swap_ref, a_ref, *refs):
    pieces, (keep_ref, send_ref) = refs[:4], refs[-2:]
    n = keep_ref.shape[0]
    swap = swap_ref[0] != 0
    coeff = jnp.concatenate([ref[...] for ref in pieces], axis=0)
    for at in range(a_ref.shape[0]):
        cols = slice(at * WIDTH, (at + 1) * WIDTH)
        product = jnp.dot(coeff, a_ref[at], preferred_element_type=F32)
        even, odd = product[:n], product[n:]
        keep_ref[:, cols] = jnp.where(swap, odd, even)
        send_ref[:, cols] = jnp.where(swap, even, odd)


def half_transform(swap, masked, even, odd, waits=()):
    count, cols, width = masked.shape
    rows = count * width
    pieces = list(even) + list(odd)
    n = len(even) * 64
    out = jax.ShapeDtypeStruct((n, rows), F32)
    return pl.pallas_call(
        half_kernel,
        out_shape=[out, out],
        in_specs=[pl.BlockSpec(memory_space=pltpu.SMEM)]
        + [pl.BlockSpec(memory_space=pltpu.VMEM)] * (1 + len(pieces))
        + [pl.BlockSpec(memory_space=pl.ANY)] * len(waits),
        out_specs=[pl.BlockSpec(memory_space=pltpu.VMEM)] * 2,
        compiler_params=params(),
        cost_estimate=cost(4 * n * rows * cols, 2 * rows * cols + 4 * n * cols + 8 * n * rows),
    )(swap, masked, *pieces, *waits)


def pack_kernel(keep_at_ref, got_at_ref, *refs):
    inputs, outs, total_ref = refs[:8], refs[8:16], refs[16]
    for at in range(4):
        for row in range(2):
            rows = slice(row * 64, (row + 1) * 64)
            total_ref[keep_at_ref[at * 2 + row]] = inputs[at * 2][rows, :]
    for at in range(4):
        for row in range(2):
            rows = slice(row * 64, (row + 1) * 64)
            total_ref[got_at_ref[at * 2 + row]] += inputs[at * 2 + 1][rows, :]
    for at in range(8):
        outs[at][...] = total_ref[at].astype(outs[at].dtype)


def pack(keep_at, got_at, pairs):
    flat = [value for pair in pairs for value in pair]
    rows = flat[0].shape[1]
    return pl.pallas_call(
        pack_kernel,
        out_shape=[jax.ShapeDtypeStruct((64, rows), F32 if at == 0 else BF16) for at in range(8)],
        in_specs=[pl.BlockSpec(memory_space=pltpu.SMEM)] * 2
        + [pl.BlockSpec(memory_space=pltpu.VMEM)] * 8,
        out_specs=[pl.BlockSpec(memory_space=pltpu.VMEM)] * 8,
        scratch_shapes=[pltpu.VMEM((8, 64, rows), F32)],
        compiler_params=params(),
        cost_estimate=cost(8 * 64 * rows, 10 * 8 * 64 * rows),
    )(keep_at, got_at, *flat)


def second_kernel(x_ref, *refs):
    gots, coeff_ref, outs, turned_ref = refs[:8], refs[8], refs[9:13], refs[13]
    half = gots[0][...]
    for ref in gots[1:]:
        half = half + ref[...].astype(F32)
    high = half.astype(BF16)
    low = (half - high.astype(F32)).astype(BF16)
    parts = []
    for slab in range(2):
        at = slice(slab * 512, (slab + 1) * 512)
        coeff = coeff_ref[slab]
        both = jnp.concatenate([high[:, at], low[:, at]], axis=0)
        product = jnp.dot(both, coeff, preferred_element_type=F32)
        parts.append(product[:64] + product[64:])
    turned_ref[...] = jnp.concatenate(parts, axis=0).T
    for dx in range(4):
        x = lax.rem(x_ref[0] + dx, 4)
        for z in range(4):
            first = pl.multiple_of((z * 4 + x) * 64, 64)
            outs[dx][z] = turned_ref[pl.ds(first, 64), :].astype(outs[dx].dtype)


def second_transform(x, gots, pq_coeff):
    return pl.pallas_call(
        second_kernel,
        out_shape=[jax.ShapeDtypeStruct((4, 64, 128), F32) for at in range(4)],
        in_specs=[pl.BlockSpec(memory_space=pltpu.SMEM)]
        + [pl.BlockSpec(memory_space=pltpu.VMEM)] * 9,
        out_specs=[pl.BlockSpec(memory_space=pltpu.VMEM)] * 4,
        scratch_shapes=[pltpu.VMEM((1024, 128), F32)],
        compiler_params=params(),
        cost_estimate=cost(8 * 64 * 512 * 1024, 4 * 1024 * 1024),
    )(x, *gots, pq_coeff)


def turn_kernel(z_ref, a_ref, b_ref, c_ref, d_ref, *outs):
    for dz in range(4):
        z = lax.rem(z_ref[0] + dz, 4)
        near = b_ref[z].astype(F32) + c_ref[z].astype(F32)
        outs[dz][...] = a_ref[z] + (near + d_ref[z].astype(F32))


def turn(z, parts):
    out = jax.ShapeDtypeStruct((64, 128), F32)
    return pl.pallas_call(
        turn_kernel,
        out_shape=[out] * 4,
        in_specs=[pl.BlockSpec(memory_space=pltpu.SMEM)]
        + [pl.BlockSpec(memory_space=pltpu.VMEM)] * 4,
        out_specs=[pl.BlockSpec(memory_space=pltpu.VMEM)] * 4,
        compiler_params=params(),
        cost_estimate=cost(4 * 64 * 128 * 4, 4 * 64 * 128 * 4 * 5),
    )(z, *parts)


def last_kernel(a_ref, b_ref, c_ref, d_ref, out_ref):
    total = (a_ref[...] + b_ref[...]) + (c_ref[...] + d_ref[...])
    out_ref[0] = total[:, :64]
    out_ref[1] = total[:, 64:]


def last(parts):
    return pl.pallas_call(
        last_kernel,
        out_shape=jax.ShapeDtypeStruct((2, 64, 64), F32),
        in_specs=[pl.BlockSpec(memory_space=pltpu.VMEM)] * 4,
        out_specs=pl.BlockSpec(memory_space=pltpu.VMEM),
        compiler_params=params(),
    )(*parts)


def body(integrals, screen, rs_coeff, pq_coeff):
    slabs, pq_rows, rs_cols = integrals.shape
    pq_at, rs_at = lax.axis_index("pq"), lax.axis_index("rs")
    z, x = pq_at // 4, pq_at % 4
    core = rs_at % 2
    sign = 1 - 2 * core
    swap = (x + core) % 2
    swap_at = swap.astype(jnp.int32).reshape(1)

    own = rs_coeff.T

    block = {(0, 0): own}
    block[0, -1] = send(own, 0, 1)
    block[-1, 0] = send(own, 1, 0)
    block[0, 1] = send(own, 0, -1)
    masked = mask(
        integrals.reshape(slabs * pq_rows, rs_cols),
        screen.reshape(slabs * (pq_rows // TILE), rs_cols // TILE),
    )
    block[0, 2] = send(block[0, -1], 0, 1)
    block[2, 0] = send(block[-1, 0], 1, 0)
    block[-1, -1] = send(after(block[-1, 0], block[0, -1]), 0, 1)
    block[-1, 1] = send(after(block[-1, 0], block[0, 1]), 0, -1)
    block[-1, 2] = send(block[-1, -1], 0, 1)
    block[1, 0] = send(after(own, block[0, 2]), -1, 0)
    first = half_transform(swap_at, masked, [own, block[0, 2]], [block[0, -1], block[0, 1]])
    block[2, -1] = send(after(block[2, 0], block[0, 2]), 0, 1)
    block[2, 1] = send(after(block[2, 0], block[-1, -1]), 0, -1)
    block[2, 2] = send(after(block[2, -1], block[-1, 2], block[-1, 1], *first), 0, 1)
    block[1, 2] = send(after(block[0, 2], block[1, 0]), -1, 0)
    block[1, -1] = send(after(block[1, 0], block[2, -1]), 0, 1)
    block[1, 1] = send(after(block[1, 0], block[2, 1]), 0, -1)
    second = half_transform(
        swap_at, masked, [block[-1, 0], block[-1, 2]], [block[-1, -1], block[-1, 1]], first
    )
    third = half_transform(
        swap_at, masked, [block[2, 0], block[2, 2]], [block[2, -1], block[2, 1]], second
    )
    fourth = half_transform(
        swap_at, masked, [block[1, 0], block[1, 2]], [block[1, -1], block[1, 1]], third
    )
    halves = [first, second, third, fourth]
    places = [((dz, even), (dz, odd)) for dz in (0, -1, 2, 1) for even, odd in ((0, -1), (2, 1))]

    def slot(place, sign):
        to = (z + sign * place[0] + 4) % 4, (x + sign * place[1] + 4) % 4
        shift = (one * (to[0] - y) + 8) % 4 * 2 + (to[1] // 2 - low + 2) % 2
        return sum(
            jnp.where(shift == dy * 2 + dl, at, 0) for at, (dy, dl) in enumerate(SHIFTS)
        )

    one = sign
    y, low = rs_at // 4, rs_at % 4 // 2
    keep_at = jnp.stack([jnp.where(swap == 0, slot(e, one), slot(o, one)) for e, o in places])
    got_at = jnp.stack([jnp.where(swap == 0, slot(e, -one), slot(o, -one)) for e, o in places])
    pairs = [(keep, core_swap(other)) for keep, other in halves]
    gots = list(pack(keep_at.astype(jnp.int32), got_at.astype(jnp.int32), pairs))
    for at in range(1, 8):
        gots[at] = rs_send(gots[at], *SHIFTS[at])
    parts = second_transform(x.astype(jnp.int32).reshape(1), gots, pq_coeff)
    parts = [parts[0]] + [pq_shift(parts[dx], 0, dx) for dx in (1, 2, 3)]
    parts = turn(z.astype(jnp.int32).reshape(1), parts)
    parts = [parts[0]] + [pq_shift(parts[dz], dz, 0) for dz in (1, 2, 3)]
    return last(parts)


def solution(mesh):
    return jax.shard_map(
        body,
        mesh=mesh,
        in_specs=(P(None, "pq", "rs"), P(None, "pq", "rs"), P("rs", "pq"), P(None, "pq", None)),
        out_specs=P(None, "pq", "rs"),
        check_vma=False,
    )
```

```python
import functools

import jax
import jax.numpy as jnp
from jax import lax
from jax.experimental import pallas as pl
from jax.experimental.pallas import tpu as pltpu
from jax.sharding import PartitionSpec as P

TILE = 128
F32 = jnp.float32
BF16 = jnp.bfloat16
VMEM_LIMIT = 14 * 1024 * 1024
WIDTH = 256


def pq_shift(value, dz, dx):
    perm = []
    for index in range(16):
        z, x = divmod(index, 4)
        perm.append((index, (z + dz) % 4 * 4 + (x + dx) % 4))
    return lax.ppermute(value, "pq", perm)


def send(value, dz, dx):
    perm = []
    for index in range(256):
        pq_at, rs_at = divmod(index, 16)
        z, x = divmod(pq_at, 4)
        sign = 1 if rs_at % 2 == 0 else -1
        perm.append((index, ((z + sign * dz) % 4 * 4 + (x + sign * dx) % 4) * 16 + rs_at))
    return lax.ppermute(value, ("pq", "rs"), perm)


def after(value, *others):
    return lax.optimization_barrier((value,) + others)[0]


SHIFTS = [(0, 0), (0, 1), (1, 0), (1, 1), (2, 0), (2, 1), (3, 0), (3, 1)]


def rs_send(value, dy, dl):
    perm = []
    for index in range(16):
        y, rest = divmod(index, 4)
        sign = 1 if index % 2 == 0 else -1
        perm.append((index, (y + sign * dy) % 4 * 4 + rest ^ (dl * 2)))
    return lax.ppermute(value, "rs", perm)


def core_swap(value):
    return lax.ppermute(value, "rs", [(index, index ^ 1) for index in range(16)])


def params():
    return pltpu.CompilerParams(vmem_limit_bytes=VMEM_LIMIT)


def cost(flops, bytes_accessed):
    return pl.CostEstimate(flops=flops, bytes_accessed=bytes_accessed, transcendentals=0)


def mask_kernel(screen_ref, a_ref, out_ref):
    at = pl.program_id(0)
    for col in range(a_ref.shape[1] // TILE):
        cols = slice(col * TILE, (col + 1) * TILE)
        for row in range(WIDTH // TILE):
            rows = slice(row * TILE, (row + 1) * TILE)
            flag = screen_ref[at * (WIDTH // TILE) + row, col].astype(F32)
            out_ref[0, cols, rows] = (a_ref[rows, cols].astype(F32) * flag).T.astype(BF16)


def mask(integrals, screen):
    rows, cols = integrals.shape
    return pl.pallas_call(
        mask_kernel,
        out_shape=jax.ShapeDtypeStruct((rows // WIDTH, cols, WIDTH), BF16),
        grid_spec=pltpu.PrefetchScalarGridSpec(
            num_scalar_prefetch=1,
            grid=(rows // WIDTH,),
            in_specs=[pl.BlockSpec((WIDTH, cols), lambda at, _: (at, 0))],
            out_specs=pl.BlockSpec((1, cols, WIDTH), lambda at, _: (at, 0, 0)),
        ),
        compiler_params=params(),
        cost_estimate=cost(rows * cols, 4 * rows * cols),
    )(screen, integrals)


def half_kernel(swap_ref, a_ref, *refs):
    pieces, (keep_ref, send_ref) = refs[:4], refs[-2:]
    n = keep_ref.shape[0]
    swap = swap_ref[0] != 0
    coeff = jnp.concatenate([ref[...] for ref in pieces], axis=0)
    for at in range(a_ref.shape[0]):
        cols = slice(at * WIDTH, (at + 1) * WIDTH)
        product = jnp.dot(coeff, a_ref[at], preferred_element_type=F32)
        even, odd = product[:n], product[n:]
        keep_ref[:, cols] = jnp.where(swap, odd, even)
        send_ref[:, cols] = jnp.where(swap, even, odd)


def half_transform(swap, masked, even, odd, waits=(), held=()):
    count, cols, width = masked.shape
    rows = count * width
    pieces = list(even) + list(odd)
    n = len(even) * 64
    out = jax.ShapeDtypeStruct((n, rows), F32)
    return pl.pallas_call(
        half_kernel,
        out_shape=[out, out],
        in_specs=[pl.BlockSpec(memory_space=pltpu.SMEM)]
        + [pl.BlockSpec(memory_space=pltpu.VMEM)] * (1 + len(pieces))
        + [pl.BlockSpec(memory_space=pl.ANY)] * len(waits)
        + [pl.BlockSpec(memory_space=pltpu.VMEM)] * len(held),
        out_specs=[pl.BlockSpec(memory_space=pltpu.VMEM)] * 2,
        compiler_params=params(),
        cost_estimate=cost(4 * n * rows * cols, 2 * rows * cols + 4 * n * cols + 8 * n * rows),
    )(swap, masked, *pieces, *waits, *held)


def pack_kernel(keep_at_ref, got_at_ref, *refs):
    inputs, outs, total_ref = refs[:8], refs[8:16], refs[16]
    for at in range(4):
        for row in range(2):
            rows = slice(row * 64, (row + 1) * 64)
            total_ref[keep_at_ref[at * 2 + row]] = inputs[at * 2][rows, :]
    for at in range(4):
        for row in range(2):
            rows = slice(row * 64, (row + 1) * 64)
            total_ref[got_at_ref[at * 2 + row]] += inputs[at * 2 + 1][rows, :]
    for at in range(8):
        outs[at][...] = total_ref[at].astype(outs[at].dtype)


def pack(keep_at, got_at, pairs):
    flat = [value for pair in pairs for value in pair]
    rows = flat[0].shape[1]
    return pl.pallas_call(
        pack_kernel,
        out_shape=[jax.ShapeDtypeStruct((64, rows), F32 if at == 0 else BF16) for at in range(8)],
        in_specs=[pl.BlockSpec(memory_space=pltpu.SMEM)] * 2
        + [pl.BlockSpec(memory_space=pltpu.VMEM)] * 8,
        out_specs=[pl.BlockSpec(memory_space=pltpu.VMEM)] * 8,
        scratch_shapes=[pltpu.VMEM((8, 64, rows), F32)],
        compiler_params=params(),
        cost_estimate=cost(8 * 64 * rows, 10 * 8 * 64 * rows),
    )(keep_at, got_at, *flat)


def second_kernel(x_ref, *refs):
    gots, coeff_ref, outs, turned_ref = refs[:8], refs[8], refs[9:13], refs[13]
    half = gots[0][...]
    for ref in gots[1:]:
        half = half + ref[...].astype(F32)
    high = half.astype(BF16)
    low = (half - high.astype(F32)).astype(BF16)
    parts = []
    for slab in range(2):
        at = slice(slab * 512, (slab + 1) * 512)
        coeff = coeff_ref[slab]
        both = jnp.concatenate([high[:, at], low[:, at]], axis=0)
        product = jnp.dot(both, coeff, preferred_element_type=F32)
        parts.append(product[:64] + product[64:])
    turned_ref[...] = jnp.concatenate(parts, axis=0).T
    for dx in range(4):
        x = lax.rem(x_ref[0] + dx, 4)
        for z in range(4):
            first = pl.multiple_of((z * 4 + x) * 64, 64)
            outs[dx][z] = turned_ref[pl.ds(first, 64), :].astype(outs[dx].dtype)


def second_transform(x, gots, pq_coeff):
    return pl.pallas_call(
        second_kernel,
        out_shape=[jax.ShapeDtypeStruct((4, 64, 128), F32) for at in range(4)],
        in_specs=[pl.BlockSpec(memory_space=pltpu.SMEM)]
        + [pl.BlockSpec(memory_space=pltpu.VMEM)] * 9,
        out_specs=[pl.BlockSpec(memory_space=pltpu.VMEM)] * 4,
        scratch_shapes=[pltpu.VMEM((1024, 128), F32)],
        compiler_params=params(),
        cost_estimate=cost(8 * 64 * 512 * 1024, 4 * 1024 * 1024),
    )(x, *gots, pq_coeff)


def turn_kernel(z_ref, a_ref, b_ref, c_ref, d_ref, *outs):
    for dz in range(4):
        z = lax.rem(z_ref[0] + dz, 4)
        near = b_ref[z].astype(F32) + c_ref[z].astype(F32)
        outs[dz][...] = a_ref[z] + (near + d_ref[z].astype(F32))


def turn(z, parts):
    out = jax.ShapeDtypeStruct((64, 128), F32)
    return pl.pallas_call(
        turn_kernel,
        out_shape=[out] * 4,
        in_specs=[pl.BlockSpec(memory_space=pltpu.SMEM)]
        + [pl.BlockSpec(memory_space=pltpu.VMEM)] * 4,
        out_specs=[pl.BlockSpec(memory_space=pltpu.VMEM)] * 4,
        compiler_params=params(),
        cost_estimate=cost(4 * 64 * 128 * 4, 4 * 64 * 128 * 4 * 5),
    )(z, *parts)


def last_kernel(a_ref, b_ref, c_ref, d_ref, out_ref):
    total = (a_ref[...] + b_ref[...]) + (c_ref[...] + d_ref[...])
    out_ref[0] = total[:, :64]
    out_ref[1] = total[:, 64:]


def last(parts):
    return pl.pallas_call(
        last_kernel,
        out_shape=jax.ShapeDtypeStruct((2, 64, 64), F32),
        in_specs=[pl.BlockSpec(memory_space=pltpu.VMEM)] * 4,
        out_specs=pl.BlockSpec(memory_space=pltpu.VMEM),
        compiler_params=params(),
    )(*parts)


def body(integrals, screen, rs_coeff, pq_coeff):
    slabs, pq_rows, rs_cols = integrals.shape
    pq_at, rs_at = lax.axis_index("pq"), lax.axis_index("rs")
    z, x = pq_at // 4, pq_at % 4
    core = rs_at % 2
    sign = 1 - 2 * core
    swap = (x + core) % 2
    swap_at = swap.astype(jnp.int32).reshape(1)

    own = rs_coeff.T

    block = {(0, 0): own}
    block[0, -1] = send(own, 0, 1)
    block[-1, 0] = send(own, 1, 0)
    block[0, 1] = send(own, 0, -1)
    masked = mask(
        integrals.reshape(slabs * pq_rows, rs_cols),
        screen.reshape(slabs * (pq_rows // TILE), rs_cols // TILE),
    )
    block[0, 2] = send(block[0, -1], 0, 1)
    block[2, 0] = send(block[-1, 0], 1, 0)
    block[-1, -1] = send(after(block[-1, 0], block[0, -1]), 0, 1)
    block[-1, 1] = send(after(block[-1, 0], block[0, 1]), 0, -1)
    block[-1, 2] = send(block[-1, -1], 0, 1)
    block[1, 0] = send(after(own, block[0, 2]), -1, 0)
    first = half_transform(swap_at, masked, [own, block[0, 2]], [block[0, -1], block[0, 1]])
    block[2, -1] = send(after(block[2, 0], block[0, 2]), 0, 1)
    block[2, 1] = send(after(block[2, 0], block[-1, -1]), 0, -1)
    block[2, 2] = send(after(block[2, -1], block[-1, 2], block[-1, 1], *first), 0, 1)
    block[1, 2] = send(after(block[0, 2], block[1, 0]), -1, 0)
    block[1, -1] = send(after(block[1, 0], block[2, -1]), 0, 1)
    block[1, 1] = send(after(block[1, 0], block[2, 1]), 0, -1)
    second = half_transform(
        swap_at, masked, [block[-1, 0], block[-1, 2]], [block[-1, -1], block[-1, 1]], first
    )
    third = half_transform(
        swap_at, masked, [block[2, 0], block[2, 2]], [block[2, -1], block[2, 1]], second, [pq_coeff]
    )
    fourth = half_transform(
        swap_at, masked, [block[1, 0], block[1, 2]], [block[1, -1], block[1, 1]], third, [pq_coeff]
    )
    halves = [first, second, third, fourth]
    places = [((dz, even), (dz, odd)) for dz in (0, -1, 2, 1) for even, odd in ((0, -1), (2, 1))]

    def slot(place, sign):
        to = (z + sign * place[0] + 4) % 4, (x + sign * place[1] + 4) % 4
        shift = (one * (to[0] - y) + 8) % 4 * 2 + (to[1] // 2 - low + 2) % 2
        return sum(
            jnp.where(shift == dy * 2 + dl, at, 0) for at, (dy, dl) in enumerate(SHIFTS)
        )

    one = sign
    y, low = rs_at // 4, rs_at % 4 // 2
    keep_at = jnp.stack([jnp.where(swap == 0, slot(e, one), slot(o, one)) for e, o in places])
    got_at = jnp.stack([jnp.where(swap == 0, slot(e, -one), slot(o, -one)) for e, o in places])
    pairs = [(keep, core_swap(other)) for keep, other in halves]
    gots = list(pack(keep_at.astype(jnp.int32), got_at.astype(jnp.int32), pairs))
    for at in range(1, 8):
        gots[at] = rs_send(gots[at], *SHIFTS[at])
    parts = second_transform(x.astype(jnp.int32).reshape(1), gots, pq_coeff)
    parts = [parts[0]] + [pq_shift(parts[dx], 0, dx) for dx in (1, 2, 3)]
    parts = turn(z.astype(jnp.int32).reshape(1), parts)
    parts = [parts[0]] + [pq_shift(parts[dz], dz, 0) for dz in (1, 2, 3)]
    return last(parts)


def solution(mesh):
    return jax.shard_map(
        body,
        mesh=mesh,
        in_specs=(P(None, "pq", "rs"), P(None, "pq", "rs"), P("rs", "pq"), P(None, "pq", None)),
        out_specs=P(None, "pq", "rs"),
        check_vma=False,
    )
```
